32 devices in a mesh: chan: 8 (over y, x, core), tm: 4 (over z).
Axes of the slice: x: 2, y: 2, z: 4, core: 2. Of those that a mesh axis runs over, the one named last changes fastest.
Arguments:
- record: bfloat16 [10240, 16384], P('chan', 'tm'), may hold values from -6 to 6
- channel_ok: int32 [10240], P('chan'), may hold values 0 or 1
- fan_bounds: int32 [2, 8193], replicated, may hold values from 0 to 5120, as said below
Outputs:
- slowness: float32 [10240, 16384], P('chan', 'tm')
The draws below stay inside these ranges and needn't reach their ends.
Inputs may be any that keep to these rules, and one draw needn't show every extreme that they name: fan_bounds[0, g] <= fan_bounds[1, g] for every g; fan_bounds[0, 0] is 0 and fan_bounds[1, 8192] is 5120.
All inputs are finite; a program needn't handle non-finite values. No bound on the sum of `channel_ok` on one device may be relied on, other than what follows from the above.
Results may differ from the reference program's by a relative error of at most 0.0063.
Values may be sent and summed in bfloat16 or wider, within the bound.
A program may use at most 192 MiB of HBM per device.

```python
import jax
import jax.numpy as jnp
from jax import lax

NC = 10240
NT = 16384
R = 4


def draw_fan_bounds(key, part):
    streams = jax.random.split(jax.random.fold_in(key, 11), 3)
    bin_count = NT // 2 + 1
    frequency = jnp.arange(bin_count, dtype=jnp.int32)
    lower_rate = jax.random.randint(streams[0], (bin_count,), 150, 260, dtype=jnp.int32)
    upper_rate = jax.random.randint(streams[1], (bin_count,), 1000, 1500, dtype=jnp.int32)
    jitter = jax.random.randint(streams[2], (bin_count,), 0, 8, dtype=jnp.int32)
    lower_bound = frequency * lower_rate // 1000 * NC // NT
    upper_bound = jnp.minimum(frequency * upper_rate // 1000 * NC // NT + jitter, NC // 2)
    return jnp.stack([lower_bound, upper_bound]).astype(jnp.int32)


def plant(entries, rng, low, high):
    longest = entries.shape.index(max(entries.shape))
    spots = []
    for shift in (0, 1):
        where = [jax.random.randint(jax.random.fold_in(rng, axis), (), 0, length) for axis, length in enumerate(entries.shape)]
        where[longest] = (where[longest] + shift) % entries.shape[longest]
        spots.append(tuple(where))
    return entries.at[spots[0]].set(low).at[spots[1]].set(high)


def level_of(key, shape, pieces, least, high):
    def one(dim, parts):
        draws = jax.random.uniform(jax.random.fold_in(jax.random.fold_in(key, 6), dim), (parts,), jnp.float32, least / len(pieces), high / len(pieces))
        return jnp.repeat(jnp.exp(draws), shape[dim] // parts).reshape((-1,) + (1,) * (len(shape) - dim - 1))

    level = one(*pieces[0])
    for cut in pieces[1:]:
        level = level * one(*cut)
    return level


def bell_draw(rng, dims, deviation, limit, pieces=(), kind=jnp.bfloat16):
    entries = jax.random.normal(rng, dims, jnp.float32) * deviation
    if len(pieces) > 0:
        entries = level_of(rng, dims, pieces, -0.22, 0.18) * entries
    return jnp.clip(entries, min=-limit, max=limit).astype(kind)


def setup_inputs(seed: int = 0) -> dict:
    streams_of = jax.random.split(jax.random.key(seed), 4)
    return {
        "record": bell_draw(streams_of[0], (NC, NT), 1.0, 6.0, ((0, 8), (1, 4))),
        "channel_ok": plant((jax.random.randint(streams_of[1], (NC,), 0, 16) < 15).astype(jnp.int32), jax.random.fold_in(streams_of[1], 1), 0, 1),
        "fan_bounds": draw_fan_bounds(jax.random.fold_in(streams_of[3], 71), 0),
    }


def rounded_parts(spectrum):
    return jnp.real(spectrum).astype(jnp.bfloat16), jnp.imag(spectrum).astype(jnp.bfloat16)


def box_sum(values, dim_index, radius):
    length = values.shape[dim_index] - 2 * radius
    running = lax.slice_in_dim(values, 0, length, axis=dim_index)
    for offset in range(1, 2 * radius + 1):
        running = running + lax.slice_in_dim(values, offset, offset + length, axis=dim_index)
    return running


def reference(record, channel_ok, fan_bounds):
    block_rows = 128
    block_cols = 128
    radius = R
    row_blocks = NC // block_rows
    cleaned = record * channel_ok.astype(jnp.bfloat16)[:, None]

    def time_part(rows_in):
        return rounded_parts(jnp.fft.fft(rows_in.astype(jnp.float32), axis=1))

    spec_re, spec_im = lax.map(time_part, cleaned.reshape(row_blocks, block_rows, NT))
    spec_re = spec_re.reshape(NC, NT)
    spec_im = spec_im.reshape(NC, NT)
    folded_table = jnp.concatenate([fan_bounds, fan_bounds[:, 1:NT // 2][:, ::-1]], axis=1)
    wave_index = jnp.arange(NC, dtype=jnp.int32)
    folded = jnp.minimum(wave_index, NC - wave_index)

    def fk_part(start_at):
        part_re = lax.dynamic_slice_in_dim(spec_re, start_at, block_cols, 1).astype(jnp.float32)
        part_im = lax.dynamic_slice_in_dim(spec_im, start_at, block_cols, 1).astype(jnp.float32)
        spectrum = jnp.fft.fft(lax.complex(part_re, part_im), axis=0)
        lower_bound = lax.dynamic_slice_in_dim(folded_table[0], start_at, block_cols, 0)
        upper_bound = lax.dynamic_slice_in_dim(folded_table[1], start_at, block_cols, 0)
        passing = (folded[:, None] >= lower_bound[None, :]) & (folded[:, None] <= upper_bound[None, :])
        kept_bins = jnp.where(passing, spectrum, jnp.zeros_like(spectrum))
        return rounded_parts(jnp.fft.ifft(kept_bins, axis=0))

    starts = jnp.arange(NT // block_cols, dtype=jnp.int32) * block_cols
    pass_re, pass_im = lax.map(fk_part, starts)
    pass_re = pass_re.transpose(1, 0, 2).reshape(row_blocks, block_rows, NT)
    pass_im = pass_im.transpose(1, 0, 2).reshape(row_blocks, block_rows, NT)

    def back_part(halves):
        signal = lax.complex(halves[0].astype(jnp.float32), halves[1].astype(jnp.float32))
        return jnp.real(jnp.fft.ifft(signal, axis=1)).astype(jnp.bfloat16)

    filtered = lax.map(back_part, (pass_re, pass_im)).reshape(NC, NT)
    rim_width = radius + 1
    padded = jnp.pad(filtered, rim_width)
    time_pos = jnp.arange(NT + 2 * radius, dtype=jnp.int32) - radius
    time_in = (time_pos >= 0) & (time_pos < NT)
    window_area = (2 * radius + 1) * (2 * radius + 1)

    def tensor_part(start_at):
        window = lax.dynamic_slice_in_dim(padded, start_at, block_rows + 2 * rim_width, 0).astype(jnp.float32)
        grad_chan = (window[2:, 1:-1] - window[:-2, 1:-1]) * 0.5
        grad_time = (window[1:-1, 2:] - window[1:-1, :-2]) * 0.5
        chan_pos = start_at - radius + jnp.arange(block_rows + 2 * radius, dtype=jnp.int32)
        chan_in = (chan_pos >= 0) & (chan_pos < NC)
        weight = (chan_in[:, None] & time_in[None, :]).astype(jnp.float32)
        products = jnp.stack([grad_chan * grad_time * weight, grad_time * grad_time * weight])
        summed = box_sum(box_sum(products, 1, radius), 2, radius)
        cross_mean = summed[0] / window_area
        along_mean = summed[1] / window_area
        return -cross_mean / (along_mean + 1e-5)

    row_starts = jnp.arange(row_blocks, dtype=jnp.int32) * block_rows
    return lax.map(tensor_part, row_starts).reshape(NC, NT)
```

```python
import math

import jax
import jax.numpy as jnp
from jax import lax
from jax.experimental import pallas as pl
from jax.experimental.pallas import tpu as pltpu
from jax.sharding import PartitionSpec as P

NC = 10240
NT = 16384
TF = 128
R = 4


def contract(pattern, left_arg, right_arg):
    return jnp.einsum(
        pattern,
        left_arg,
        right_arg,
        precision=lax.Precision.HIGH,
        preferred_element_type=jnp.float32,
    )


def rotations(row_digits, col_digits, length):
    phase_int = row_digits[:, None] * col_digits[None, :] % length
    angles = phase_int.astype(jnp.float32) * (2.0 * math.pi / length)
    return (jnp.cos(angles), jnp.sin(angles))


def split_hi_lo(values):
    high = values.astype(jnp.bfloat16)
    low = (values - high.astype(jnp.float32)).astype(jnp.bfloat16)
    return high, low


def dot(left, right):
    return jnp.dot(left, right, preferred_element_type=jnp.float32)


def forward_kernel(x_ref, w_ref, tc_ref, ts_ref, b_ref, o_ref, held):
    rows = held.shape[0]
    half = TF // 2

    def one(row, carry):
        x = x_ref[:, pl.ds(row, 1)].reshape(TF, TF)
        first = dot(w_ref[...], jnp.concatenate([x, x], axis=0))
        first_re, first_im = first[:TF], first[TF:]
        tw_cos, tw_sin = tc_ref[...], ts_ref[...]
        turned_re = first_re * tw_cos + first_im * tw_sin
        turned_im = first_im * tw_cos - first_re * tw_sin
        high, low = split_hi_lo(jnp.concatenate([turned_re, turned_im], axis=1))
        wide = dot(high, b_ref[...])
        spec = wide[:, :TF] + wide[:, TF:] + dot(low, b_ref[:, :TF])
        lane = lax.broadcasted_iota(jnp.int32, (8, TF), 1)
        line = lax.broadcasted_iota(jnp.int32, (8, TF), 0)
        signs = jnp.where(lane % 2 == 0, 1.0, -1.0)
        highest = jnp.sum(turned_re[:8] * signs, axis=1, keepdims=True)
        top = jnp.where((lane == half) & (line == 0), highest, spec[:8])
        held[pl.ds(row, 1)] = jnp.concatenate([top, spec[8:]], axis=0)[None]
        return carry

    lax.fori_loop(0, rows, one, 0, unroll=4)
    o_ref[...] = jnp.swapaxes(held[...], 0, 1).astype(jnp.bfloat16)


def time_forward(series):
    blocks, row_count, depth, _ = series.shape
    rows = 16
    half = TF // 2
    digits = jnp.arange(TF, dtype=jnp.int32)
    cos_w, sin_w = rotations(digits, digits, TF)
    tw_cos, tw_sin = rotations(digits, digits, TF * TF)
    w_high, w_low = split_hi_lo(jnp.concatenate([cos_w, -sin_w], axis=0))
    w = jnp.concatenate([w_high, w_low], axis=1)
    cos_k, sin_k = cos_w[:, :half], sin_w[:, :half]
    b = jnp.concatenate(
        [
            jnp.concatenate([cos_k, -sin_k], axis=1),
            jnp.concatenate([sin_k, cos_k], axis=1),
        ],
        axis=0,
    )
    b = jnp.concatenate(split_hi_lo(b), axis=1)
    whole = lambda i: (0, 0)
    return pl.pallas_call(
        forward_kernel,
        grid=(row_count // rows,),
        in_specs=[
            pl.BlockSpec((blocks, rows, depth, TF), lambda i: (0, i, 0, 0)),
            pl.BlockSpec(w.shape, whole),
            pl.BlockSpec((TF, TF), whole),
            pl.BlockSpec((TF, TF), whole),
            pl.BlockSpec(b.shape, whole),
        ],
        out_specs=pl.BlockSpec((TF, rows, TF), lambda i: (0, i, 0)),
        out_shape=jax.ShapeDtypeStruct((TF, row_count, TF), jnp.bfloat16),
        scratch_shapes=[pltpu.VMEM((rows, TF, TF), jnp.float32)],
        compiler_params=pltpu.CompilerParams(vmem_limit_bytes=48 * 2**20),
        name="time_forward",
    )(series, w, tw_cos, tw_sin, b)


def inverse_kernel(p_ref, b_ref, tc_ref, ts_ref, w_ref, o_ref, held):
    rows = held.shape[0]
    blocks, _, depth, _ = o_ref.shape
    half = TF // 2
    held[...] = jnp.swapaxes(p_ref[...].astype(jnp.float32), 0, 1)

    def one(row, carry):
        part = held[pl.ds(row, 1)].reshape(TF, TF)
        packed = part.astype(jnp.bfloat16)
        mixed = dot(jnp.concatenate([packed, packed], axis=1), b_ref[...])
        mixed_re, mixed_im = mixed[:, :TF], mixed[:, TF:]
        lane = lax.broadcasted_iota(jnp.int32, (8, TF), 1)
        line = lax.broadcasted_iota(jnp.int32, (8, TF), 0)
        signs = jnp.where(lane % 2 == 0, 0.5, -0.5)
        fix = signs * part[:8, half : half + 1] - 0.5 * part[:8, 0:1]
        top = mixed_re[:8] + jnp.where(line == 0, fix, 0.0)
        mixed_re = jnp.concatenate([top, mixed_re[8:]], axis=0)
        tw_cos, tw_sin = tc_ref[...], ts_ref[...]
        turned_re = mixed_re * tw_cos - mixed_im * tw_sin
        turned_im = mixed_im * tw_cos + mixed_re * tw_sin
        high, low = split_hi_lo(jnp.concatenate([turned_re, turned_im], axis=0))
        tall = dot(w_ref[...], high)
        out = tall[:TF] + tall[TF:] + dot(w_ref[:TF, :], low)
        o_ref[:, pl.ds(row, 1)] = out.reshape(blocks, 1, depth, TF).astype(jnp.bfloat16)
        return carry

    lax.fori_loop(0, rows, one, 0, unroll=4)


def time_inverse(spec, blocks):
    row_count = spec.shape[1]
    rows = 16
    half = TF // 2
    depth = TF // blocks
    digits = jnp.arange(TF, dtype=jnp.int32)
    cos_w, sin_w = rotations(digits, digits, TF)
    tw_cos, tw_sin = rotations(digits, digits, TF * TF)
    scale = 2.0 / (TF * TF)
    cos_j, sin_j = cos_w[:half], sin_w[:half]
    b = jnp.concatenate(
        [
            jnp.concatenate([cos_j, sin_j], axis=1),
            jnp.concatenate([-sin_j, cos_j], axis=1),
        ],
        axis=0,
    )
    b = jnp.concatenate(split_hi_lo(b), axis=0)
    w = jnp.concatenate(split_hi_lo(jnp.concatenate([cos_w, -sin_w], axis=1)), axis=0)
    whole = lambda i: (0, 0)
    return pl.pallas_call(
        inverse_kernel,
        grid=(row_count // rows,),
        in_specs=[
            pl.BlockSpec((TF, rows, TF), lambda i: (0, i, 0)),
            pl.BlockSpec(b.shape, whole),
            pl.BlockSpec((TF, TF), whole),
            pl.BlockSpec((TF, TF), whole),
            pl.BlockSpec(w.shape, whole),
        ],
        out_specs=pl.BlockSpec((blocks, rows, depth, TF), lambda i: (0, i, 0, 0)),
        out_shape=jax.ShapeDtypeStruct((blocks, row_count, depth, TF), jnp.bfloat16),
        scratch_shapes=[pltpu.VMEM((rows, TF, TF), jnp.float32)],
        compiler_params=pltpu.CompilerParams(vmem_limit_bytes=48 * 2**20),
        name="time_inverse",
    )(spec, b, tw_cos * scale, tw_sin * scale, w)


def reversed_waves(values):
    along_outer = jnp.roll(jnp.flip(values, 0), 1, axis=0)
    along_inner = jnp.flip(along_outer, 1)
    first_row = jnp.roll(along_inner[0:1], 1, axis=1)
    return jnp.concatenate([first_row, along_inner[1:]], axis=0)


def channel_filter(
    pencil_re, pencil_im, position, lower_bound, upper_bound, top_low, top_high, packed
):
    devices = position.shape[0]
    row_depth = NC // devices
    columns = pencil_re.shape[1]
    part_re = pencil_re.astype(jnp.float32).reshape(devices, row_depth, columns)
    part_im = pencil_im.astype(jnp.float32).reshape(devices, row_depth, columns)
    outer_digits = jnp.arange(devices, dtype=jnp.int32)
    inner_digits = jnp.arange(row_depth, dtype=jnp.int32)
    cos_a, sin_a = rotations(outer_digits, position, devices)
    cos_b, sin_b = rotations(inner_digits, inner_digits, row_depth)
    tw_cos, tw_sin = rotations(outer_digits, inner_digits, NC)
    tw_cos = tw_cos[:, :, None]
    tw_sin = tw_sin[:, :, None]
    first_re = contract("pbf,kp->kbf", part_re, cos_a) + contract("pbf,kp->kbf", part_im, sin_a)
    first_im = contract("pbf,kp->kbf", part_im, cos_a) - contract("pbf,kp->kbf", part_re, sin_a)
    turned_re = first_re * tw_cos + first_im * tw_sin
    turned_im = first_im * tw_cos - first_re * tw_sin
    wave_re = contract("kbf,jb->kjf", turned_re, cos_b) + contract("kbf,jb->kjf", turned_im, sin_b)
    wave_im = contract("kbf,jb->kjf", turned_im, cos_b) - contract("kbf,jb->kjf", turned_re, sin_b)
    number = outer_digits[:, None] + devices * inner_digits[None, :]
    folded = jnp.minimum(number, NC - number)
    passing = (
        (folded[:, :, None] >= lower_bound[None, None, :])
        & (folded[:, :, None] <= upper_bound[None, None, :])
    ).astype(jnp.float32)
    top_pass = ((folded >= top_low) & (folded <= top_high)).astype(jnp.float32)
    first_pass = passing[:, :, 0]
    column_re = wave_re[:, :, 0]
    column_im = wave_im[:, :, 0]
    mirror_re = reversed_waves(column_re)
    mirror_im = reversed_waves(column_im)
    even_part = (first_pass + top_pass) * 0.5
    odd_part = (first_pass - top_pass) * 0.5
    split_re = even_part * column_re + odd_part * mirror_re
    split_im = even_part * column_im - odd_part * mirror_im
    wave_re = wave_re * passing
    wave_im = wave_im * passing
    wave_re = wave_re.at[:, :, 0].set(packed * split_re + (1.0 - packed) * wave_re[:, :, 0])
    wave_im = wave_im.at[:, :, 0].set(packed * split_im + (1.0 - packed) * wave_im[:, :, 0])
    back_re = contract("kjf,jb->kbf", wave_re, cos_b) - contract("kjf,jb->kbf", wave_im, sin_b)
    back_im = contract("kjf,jb->kbf", wave_im, cos_b) + contract("kjf,jb->kbf", wave_re, sin_b)
    untwist_re = back_re * tw_cos - back_im * tw_sin
    untwist_im = back_im * tw_cos + back_re * tw_sin
    out_re = contract("kbf,kp->pbf", untwist_re, cos_a) - contract("kbf,kp->pbf", untwist_im, sin_a)
    out_im = contract("kbf,kp->pbf", untwist_im, cos_a) + contract("kbf,kp->pbf", untwist_re, sin_a)
    return (
        (out_re / NC).reshape(NC, columns).astype(jnp.bfloat16),
        (out_im / NC).reshape(NC, columns).astype(jnp.bfloat16),
    )


EDGE = 16
SIDE = 128


def tensor_kernel(
    where_ref, above_ref, mid_ref, below_ref, head_ref, foot_ref, left_ref, right_ref, o_ref
):
    step = pl.program_id(0)
    steps = pl.num_programs(0)
    rows, width = mid_ref.shape
    tall = rows + 2 * EDGE
    chunk = 512
    for start in range(0, width, chunk):
        low, high = start - SIDE, start + chunk + SIDE
        inner = slice(max(low, 0), min(high, width))
        above = jnp.where(step == 0, head_ref[:, inner], above_ref[:, inner])
        below = jnp.where(step == steps - 1, foot_ref[:, inner], below_ref[:, inner])
        cells = jnp.concatenate([above, mid_ref[:, inner], below], axis=0).astype(jnp.float32)
        pieces = [cells]
        lines = pl.ds(pl.multiple_of(step * rows, 16), tall)
        if low < 0:
            pieces = [left_ref[lines, :].astype(jnp.float32)] + pieces
        if high > width:
            pieces = pieces + [right_ref[lines, :].astype(jnp.float32)]
        cells = jnp.concatenate(pieces, axis=1) if len(pieces) > 1 else cells
        wide = cells.shape[1]
        row_at = where_ref[0] + step * rows - EDGE + lax.broadcasted_iota(jnp.int32, (tall, 1), 0)
        col_at = where_ref[1] + low + lax.broadcasted_iota(jnp.int32, (1, wide), 1)
        inside = ((row_at >= 0) & (row_at < NC)) & ((col_at >= 0) & (col_at < NT))
        grad_chan = pltpu.roll(cells, tall - 1, 0) - pltpu.roll(cells, 1, 0)
        grad_time = pltpu.roll(cells, wide - 1, 1) - pltpu.roll(cells, 1, 1)
        grad_time = jnp.where(inside, grad_time, 0.0)

        def box(values, axis):
            length = values.shape[axis]
            two = values + pltpu.roll(values, 1, axis)
            four = two + pltpu.roll(two, 2, axis)
            eight = four + pltpu.roll(four, length - R, axis)
            return eight + pltpu.roll(values, R, axis)

        def smooth(values):
            return box(box(values, 0)[EDGE : EDGE + rows], 1)[:, SIDE : SIDE + chunk]

        cross = smooth(grad_chan * grad_time)
        along = smooth(grad_time * grad_time)
        area = (2 * R + 1) * (2 * R + 1)
        o_ref[:, start : start + chunk] = -cross / (along + 4e-5 * area)


def from_before(values, axis):
    count = lax.axis_size(axis)
    return lax.ppermute(values, axis, [(i, i + 1) for i in range(count - 1)])


def from_after(values, axis):
    count = lax.axis_size(axis)
    return lax.ppermute(values, axis, [(i + 1, i) for i in range(count - 1)])


def tensor_slowness(cells):
    tile_chan, tile_time = cells.shape
    head = from_before(cells[tile_chan - EDGE :], "chan")
    foot = from_after(cells[:EDGE], "chan")

    def strip(cols):
        return jnp.concatenate([head[:, cols], cells[:, cols], foot[:, cols]], axis=0)

    left = from_before(strip(slice(tile_time - SIDE, tile_time)), "tm")
    right = from_after(strip(slice(0, SIDE)), "tm")
    where = jnp.stack(
        [lax.axis_index("chan") * tile_chan, lax.axis_index("tm") * tile_time]
    ).astype(jnp.int32)
    rows = 64
    ratio = rows // EDGE
    last = tile_chan // EDGE - 1
    whole = lambda i: (0, 0)
    return pl.pallas_call(
        tensor_kernel,
        grid=(tile_chan // rows,),
        in_specs=[
            pl.BlockSpec(memory_space=pltpu.SMEM),
            pl.BlockSpec((EDGE, tile_time), lambda i: (jnp.maximum(i * ratio - 1, 0), 0)),
            pl.BlockSpec((rows, tile_time), lambda i: (i, 0)),
            pl.BlockSpec((EDGE, tile_time), lambda i: (jnp.minimum((i + 1) * ratio, last), 0)),
            pl.BlockSpec((EDGE, tile_time), whole),
            pl.BlockSpec((EDGE, tile_time), whole),
            pl.BlockSpec((tile_chan + 2 * EDGE, SIDE), whole),
            pl.BlockSpec((tile_chan + 2 * EDGE, SIDE), whole),
        ],
        out_specs=pl.BlockSpec((rows, tile_time), lambda i: (i, 0)),
        out_shape=jax.ShapeDtypeStruct((tile_chan, tile_time), jnp.float32),
        compiler_params=pltpu.CompilerParams(vmem_limit_bytes=48 * 2**20),
        name="tensor_slowness",
    )(where, cells, cells, cells, head, foot, left, right)


def per_device(record, channel_ok, fan_bounds):
    chan_count = lax.axis_size("chan")
    time_count = lax.axis_size("tm")
    devices = chan_count * time_count
    tile_chan, tile_time = record.shape
    row_count = tile_chan // time_count
    half = TF // 2
    digits = TF // devices
    tiles = record * channel_ok.astype(jnp.bfloat16)[:, None]
    tiles = tiles.reshape(time_count, row_count, tile_time // TF, TF)
    series = lax.all_to_all(tiles, "tm", split_axis=0, concat_axis=0)
    block_index = lax.axis_index("chan") * time_count + lax.axis_index("tm")
    top_low = fan_bounds[0, NT // 2]
    top_high = fan_bounds[1, NT // 2]
    columns = digits * half
    ordered = (
        fan_bounds[:, : NT // 2].reshape(2, TF // 2, TF).transpose(0, 2, 1).reshape(2, NT // 2)
    )
    packed = (block_index == 0).astype(jnp.float32)
    window = lax.dynamic_slice_in_dim(ordered, block_index * columns, columns, 1)
    slot_index = jnp.arange(devices, dtype=jnp.int32)
    spec = time_forward(series).reshape(devices, digits, row_count, TF)
    pencil = lax.all_to_all(spec, ("chan", "tm"), split_axis=0, concat_axis=0)

    def flat(part):
        return part.transpose(0, 2, 1, 3).reshape(NC, columns)

    def folded(part):
        return part.reshape(devices, row_count, digits, half).transpose(0, 2, 1, 3)

    filt_re, filt_im = channel_filter(
        flat(pencil[..., :half]),
        flat(pencil[..., half:]),
        slot_index,
        window[0],
        window[1],
        top_low,
        top_high,
        packed,
    )
    filt = jnp.concatenate([folded(filt_re), folded(filt_im)], axis=3)
    back = lax.all_to_all(filt, ("chan", "tm"), split_axis=0, concat_axis=0)
    rows = time_inverse(back.reshape(TF, row_count, TF), time_count)
    rows = lax.all_to_all(rows, "tm", split_axis=0, concat_axis=0)
    return tensor_slowness(rows.reshape(tile_chan, tile_time))


def solution(mesh):
    in_specs = (P("chan", "tm"), P("chan"), P())
    out_specs = P("chan", "tm")
    return jax.shard_map(
        per_device, mesh=mesh, in_specs=in_specs, out_specs=out_specs, check_vma=False
    )
```

```python
import functools
import math

import jax
import jax.numpy as jnp
from jax import lax
from jax.experimental import pallas as pl
from jax.experimental.pallas import tpu as pltpu
from jax.sharding import PartitionSpec as P

NC = 10240
NT = 16384
TF = 128
R = 4


def rotations(row_digits, col_digits, length):
    phase_int = row_digits[:, None] * col_digits[None, :] % length
    angles = phase_int.astype(jnp.float32) * (2.0 * math.pi / length)
    return (jnp.cos(angles), jnp.sin(angles))


def split_hi_lo(values):
    high = values.astype(jnp.bfloat16)
    low = (values - high.astype(jnp.float32)).astype(jnp.bfloat16)
    return high, low


def dot(left, right):
    return jnp.dot(left, right, preferred_element_type=jnp.float32)


def split_table(values):
    high = lax.reduce_precision(values, 8, 7)
    return high.astype(jnp.bfloat16), (values - high).astype(jnp.bfloat16)


def forward_kernel(x_ref, w_ref, tc_ref, ts_ref, b_ref, o_ref, held):
    rows = held.shape[0]
    half = TF // 2

    def one(row, carry):
        x = x_ref[:, pl.ds(row, 1)].reshape(TF, TF)
        first = dot(w_ref[...], jnp.concatenate([x, x], axis=0))
        first_re, first_im = first[:TF], first[TF:]
        tw_cos, tw_sin = tc_ref[...], ts_ref[...]
        turned_re = first_re * tw_cos + first_im * tw_sin
        turned_im = first_im * tw_cos - first_re * tw_sin
        high, low = split_hi_lo(jnp.concatenate([turned_re, turned_im], axis=1))
        wide = dot(high, b_ref[...])
        spec = wide[:, :TF] + wide[:, TF:] + dot(low, b_ref[:, :TF])
        lane = lax.broadcasted_iota(jnp.int32, (8, TF), 1)
        line = lax.broadcasted_iota(jnp.int32, (8, TF), 0)
        signs = jnp.where(lane % 2 == 0, 1.0, -1.0)
        highest = jnp.sum(turned_re[:8] * signs, axis=1, keepdims=True)
        top = jnp.where((lane == half) & (line == 0), highest, spec[:8])
        held[pl.ds(row, 1)] = jnp.concatenate([top, spec[8:]], axis=0)[None]
        return carry

    lax.fori_loop(0, rows, one, 0, unroll=4)
    o_ref[...] = jnp.swapaxes(held[...], 0, 1).astype(jnp.bfloat16)


def time_forward(series):
    blocks, row_count, depth, _ = series.shape
    rows = 16
    half = TF // 2
    digits = jnp.arange(TF, dtype=jnp.int32)
    cos_w, sin_w = rotations(digits, digits, TF)
    tw_cos, tw_sin = rotations(digits, digits, TF * TF)
    w_high, w_low = split_table(jnp.concatenate([cos_w, -sin_w], axis=0))
    w = jnp.concatenate([w_high, w_low], axis=1)
    cos_k, sin_k = cos_w[:, :half], sin_w[:, :half]
    b = jnp.concatenate(
        [
            jnp.concatenate([cos_k, -sin_k], axis=1),
            jnp.concatenate([sin_k, cos_k], axis=1),
        ],
        axis=0,
    )
    b = jnp.concatenate(split_table(b), axis=1)
    whole = lambda i: (0, 0)
    return pl.pallas_call(
        forward_kernel,
        grid=(row_count // rows,),
        in_specs=[
            pl.BlockSpec((blocks, rows, depth, TF), lambda i: (0, i, 0, 0)),
            pl.BlockSpec(w.shape, whole),
            pl.BlockSpec((TF, TF), whole),
            pl.BlockSpec((TF, TF), whole),
            pl.BlockSpec(b.shape, whole),
        ],
        out_specs=pl.BlockSpec((TF, rows, TF), lambda i: (0, i, 0)),
        out_shape=jax.ShapeDtypeStruct((TF, row_count, TF), jnp.bfloat16),
        scratch_shapes=[pltpu.VMEM((rows, TF, TF), jnp.float32)],
        compiler_params=pltpu.CompilerParams(vmem_limit_bytes=48 * 2**20),
        name="time_forward",
    )(series, w, tw_cos, tw_sin, b)


def inverse_kernel(p_ref, b_ref, tc_ref, ts_ref, w_ref, o_ref, held):
    rows = held.shape[0]
    blocks, _, depth, _ = o_ref.shape
    half = TF // 2
    held[...] = jnp.swapaxes(p_ref[...].astype(jnp.float32), 0, 1)

    def one(row, carry):
        part = held[pl.ds(row, 1)].reshape(TF, TF)
        packed = part.astype(jnp.bfloat16)
        mixed = dot(jnp.concatenate([packed, packed], axis=1), b_ref[...])
        mixed_re, mixed_im = mixed[:, :TF], mixed[:, TF:]
        lane = lax.broadcasted_iota(jnp.int32, (8, TF), 1)
        line = lax.broadcasted_iota(jnp.int32, (8, TF), 0)
        signs = jnp.where(lane % 2 == 0, 0.5, -0.5)
        fix = signs * part[:8, half : half + 1] - 0.5 * part[:8, 0:1]
        top = mixed_re[:8] + jnp.where(line == 0, fix, 0.0)
        mixed_re = jnp.concatenate([top, mixed_re[8:]], axis=0)
        tw_cos, tw_sin = tc_ref[...], ts_ref[...]
        turned_re = mixed_re * tw_cos - mixed_im * tw_sin
        turned_im = mixed_im * tw_cos + mixed_re * tw_sin
        high, low = split_hi_lo(jnp.concatenate([turned_re, turned_im], axis=0))
        tall = dot(w_ref[...], high)
        out = tall[:TF] + tall[TF:] + dot(w_ref[:TF, :], low)
        o_ref[:, pl.ds(row, 1)] = out.reshape(blocks, 1, depth, TF).astype(jnp.bfloat16)
        return carry

    lax.fori_loop(0, rows, one, 0, unroll=4)


def time_inverse(spec, blocks):
    row_count = spec.shape[1]
    rows = 16
    half = TF // 2
    depth = TF // blocks
    digits = jnp.arange(TF, dtype=jnp.int32)
    cos_w, sin_w = rotations(digits, digits, TF)
    tw_cos, tw_sin = rotations(digits, digits, TF * TF)
    scale = 2.0 / (TF * TF)
    cos_j, sin_j = cos_w[:half], sin_w[:half]
    b = jnp.concatenate(
        [
            jnp.concatenate([cos_j, sin_j], axis=1),
            jnp.concatenate([-sin_j, cos_j], axis=1),
        ],
        axis=0,
    )
    b = jnp.concatenate(split_table(b), axis=0)
    w = jnp.concatenate(split_table(jnp.concatenate([cos_w, -sin_w], axis=1)), axis=0)
    whole = lambda i: (0, 0)
    return pl.pallas_call(
        inverse_kernel,
        grid=(row_count // rows,),
        in_specs=[
            pl.BlockSpec((TF, rows, TF), lambda i: (0, i, 0)),
            pl.BlockSpec(b.shape, whole),
            pl.BlockSpec((TF, TF), whole),
            pl.BlockSpec((TF, TF), whole),
            pl.BlockSpec(w.shape, whole),
        ],
        out_specs=pl.BlockSpec((blocks, rows, depth, TF), lambda i: (0, i, 0, 0)),
        out_shape=jax.ShapeDtypeStruct((blocks, row_count, depth, TF), jnp.bfloat16),
        scratch_shapes=[pltpu.VMEM((rows, TF, TF), jnp.float32)],
        compiler_params=pltpu.CompilerParams(vmem_limit_bytes=48 * 2**20),
        name="time_inverse",
    )(spec, b, tw_cos * scale, tw_sin * scale, w)


def quarter_turn(values):
    width = values.shape[-1]
    lane = lax.broadcasted_iota(jnp.int32, (1, width), 1)
    return pltpu.roll(values, width // 2, 1) * jnp.where(lane < width // 2, 1.0, -1.0)


def fast_fourier(parts, sign):
    count = len(parts)
    if count == 1:
        return parts
    even = fast_fourier(parts[0::2], sign)
    odd = fast_fourier(parts[1::2], sign)
    low, high = [], []
    for k in range(count // 2):
        if k == 0:
            turned = odd[k]
        elif 4 * k == count:
            turned = quarter_turn(odd[k]) * sign
        else:
            angle = 2.0 * math.pi * k / count
            turned = odd[k] * math.cos(angle) + quarter_turn(odd[k]) * (sign * math.sin(angle))
        low.append(even[k] + turned)
        high.append(even[k] - turned)
    return low + high


def channel_kernel(sizes, flag_ref, bound_ref, tc_ref, ts_ref, f_ref, g_ref, *refs):
    x_refs, o_refs, held = refs[: len(sizes)], refs[len(sizes) : -1], refs[-1]
    count, depth, width = held.shape
    step = pl.program_id(0)
    first = flag_ref[0] == 1
    half = width // 2
    lane = lax.broadcasted_iota(jnp.int32, (1, width), 1)
    lines = 16

    def transform(matrix_ref, values):
        high, low = split_hi_lo(jnp.concatenate([values, quarter_turn(values)], axis=0))
        wide = dot(matrix_ref[:depth], jnp.concatenate([high, low], axis=1))
        return wide[:, :width] + wide[:, width:] + dot(matrix_ref[depth:], high)

    @pl.when((step > 0) | first)
    def _():
        drop = jnp.where((step == 1) & first, 1.0, 0.0)
        kept = jnp.where(
            step == 0,
            (lane == 0).astype(jnp.float32),
            1.0 - drop * (lane == half).astype(jnp.float32),
        )

        def gather(x_ref, offset, index, carry):
            here = pl.ds(pl.multiple_of(index * lines, lines), lines)
            there = pl.ds(pl.multiple_of(offset + index * lines, lines), lines)
            parts = []
            for p in range(count):
                part = x_ref[p, 0, here, :].astype(jnp.float32)
                parts.append(jnp.where(step == 0, pltpu.roll(part, half, 1), part) * kept)
            for p, part in enumerate(fast_fourier(parts, 1.0)):
                held[p, there, :] = part
            return carry

        offset = 0
        for x_ref, size in zip(x_refs, sizes):
            lax.fori_loop(0, size // lines, functools.partial(gather, x_ref, offset), 0)
            offset += size
        lower, upper = bound_ref[0, 0:1, :], bound_ref[0, 1:2, :]

        def middle(outer, carry):
            turn_cos, turn_sin = tc_ref[outer], ts_ref[outer]
            values = held[outer]
            values = values * turn_cos + pltpu.roll(values, half, 1) * turn_sin
            wave = transform(f_ref, values)
            number = outer + count * lax.broadcasted_iota(jnp.int32, (depth, width), 0)
            folded = jnp.minimum(number, count * depth - number)
            wave = jnp.where((folded >= lower) & (folded <= upper), wave, 0.0)
            back = transform(g_ref, wave)
            held[outer] = back * turn_cos - pltpu.roll(back, half, 1) * turn_sin
            return carry

        lax.fori_loop(0, count, middle, 0)
        placed = lane == jnp.where((step == 1) & first, half, -1)

        def scatter(o_ref, offset, index, carry):
            here = pl.ds(pl.multiple_of(index * lines, lines), lines)
            there = pl.ds(pl.multiple_of(offset + index * lines, lines), lines)
            parts = fast_fourier([held[p, there, :] for p in range(count)], -1.0)
            for p, part in enumerate(parts):
                part = part * (1.0 / (count * depth))
                part = jnp.where(step == 0, pltpu.roll(part, half, 1), part)
                before = o_ref[p, 0, here, :].astype(jnp.float32)
                o_ref[p, 0, here, :] = jnp.where(placed, before, part).astype(jnp.bfloat16)
            return carry

        offset = 0
        for o_ref, size in zip(o_refs, sizes):
            lax.fori_loop(0, size // lines, functools.partial(scatter, o_ref, offset), 0)
            offset += size


def channel_filter(pencils, bounds, packed):
    count, digits, _, width = pencils[0].shape
    sizes = [pencil.shape[2] for pencil in pencils]
    depth = sum(sizes)
    outer = jnp.arange(count, dtype=jnp.int32)
    inner = jnp.arange(depth, dtype=jnp.int32)
    cos_b, sin_b = rotations(inner, inner, depth)
    tw_cos, tw_sin = rotations(outer, inner, count * depth)
    signs = jnp.where(jnp.arange(width) < width // 2, 1.0, -1.0).astype(jnp.float32)
    tw_cos = jnp.broadcast_to(tw_cos[:, :, None], (count, depth, width))
    tw_sin = tw_sin[:, :, None] * signs
    ahead = jnp.concatenate(split_table(jnp.concatenate([cos_b, sin_b], axis=1)), axis=0)
    behind = jnp.concatenate(split_table(jnp.concatenate([cos_b, -sin_b], axis=1)), axis=0)
    once = pl.Buffered(1)
    flat = lambda s: (0, 0)
    solid = lambda s: (0, 0, 0)
    at = lambda s: (0, jnp.maximum(s - 1, 0), 0, 0)
    blocks = [pl.BlockSpec((count, 1, size, width), at) for size in sizes]
    return pl.pallas_call(
        functools.partial(channel_kernel, sizes),
        grid=(digits + 1,),
        in_specs=[
            pl.BlockSpec(memory_space=pltpu.SMEM),
            pl.BlockSpec((1, 8, width), lambda s: (s, 0, 0)),
            pl.BlockSpec(tw_cos.shape, solid, pipeline_mode=once),
            pl.BlockSpec(tw_sin.shape, solid, pipeline_mode=once),
            pl.BlockSpec(ahead.shape, flat, pipeline_mode=once),
            pl.BlockSpec(behind.shape, flat, pipeline_mode=once),
        ]
        + blocks,
        out_specs=blocks,
        out_shape=[jax.ShapeDtypeStruct(pencil.shape, jnp.bfloat16) for pencil in pencils],
        scratch_shapes=[pltpu.VMEM((count, depth, width), jnp.float32)],
        compiler_params=pltpu.CompilerParams(vmem_limit_bytes=56 * 2**20),
        name="channel_filter",
    )(packed, bounds, tw_cos, tw_sin, ahead, behind, *pencils)


def step_bounds(window, top):
    digits = window.shape[1]
    wide = jnp.concatenate([window, window], axis=2)
    above = jnp.broadcast_to(top[:, None, None], (2, 1, wide.shape[2]))
    bounds = jnp.concatenate([above, wide], axis=1).transpose(1, 0, 2)
    return jnp.pad(bounds, ((0, 0), (0, 6), (0, 0)))


EDGE = 16
SIDE = 128


def tensor_kernel(
    where_ref, above_ref, mid_ref, below_ref, head_ref, foot_ref, left_ref, right_ref, o_ref
):
    step = pl.program_id(0)
    steps = pl.num_programs(0)
    rows, width = mid_ref.shape
    tall = rows + 2 * EDGE
    chunk = 512
    for start in range(0, width, chunk):
        low, high = start - SIDE, start + chunk + SIDE
        inner = slice(max(low, 0), min(high, width))
        above = jnp.where(step == 0, head_ref[:, inner], above_ref[:, inner])
        below = jnp.where(step == steps - 1, foot_ref[:, inner], below_ref[:, inner])
        cells = jnp.concatenate([above, mid_ref[:, inner], below], axis=0).astype(jnp.float32)
        pieces = [cells]
        lines = pl.ds(pl.multiple_of(step * rows, 16), tall)
        if low < 0:
            pieces = [left_ref[lines, :].astype(jnp.float32)] + pieces
        if high > width:
            pieces = pieces + [right_ref[lines, :].astype(jnp.float32)]
        cells = jnp.concatenate(pieces, axis=1) if len(pieces) > 1 else cells
        wide = cells.shape[1]
        row_at = where_ref[0] + step * rows - EDGE + lax.broadcasted_iota(jnp.int32, (tall, 1), 0)
        col_at = where_ref[1] + low + lax.broadcasted_iota(jnp.int32, (1, wide), 1)
        inside = ((row_at >= 0) & (row_at < NC)) & ((col_at >= 0) & (col_at < NT))
        grad_chan = pltpu.roll(cells, tall - 1, 0) - pltpu.roll(cells, 1, 0)
        grad_time = pltpu.roll(cells, wide - 1, 1) - pltpu.roll(cells, 1, 1)
        grad_time = jnp.where(inside, grad_time, 0.0)

        def box(values, axis):
            length = values.shape[axis]
            two = values + pltpu.roll(values, 1, axis)
            four = two + pltpu.roll(two, 2, axis)
            eight = four + pltpu.roll(four, length - R, axis)
            return eight + pltpu.roll(values, R, axis)

        def smooth(values):
            return box(box(values, 0)[EDGE : EDGE + rows], 1)[:, SIDE : SIDE + chunk]

        cross = smooth(grad_chan * grad_time)
        along = smooth(grad_time * grad_time)
        area = (2 * R + 1) * (2 * R + 1)
        o_ref[:, start : start + chunk] = -cross / (along + 4e-5 * area)


def from_before(values, axis):
    count = lax.axis_size(axis)
    return lax.ppermute(values, axis, [(i, i + 1) for i in range(count - 1)])


def from_after(values, axis):
    count = lax.axis_size(axis)
    return lax.ppermute(values, axis, [(i + 1, i) for i in range(count - 1)])


def tensor_slowness(cells):
    tile_chan, tile_time = cells.shape
    head = from_before(cells[tile_chan - EDGE :], "chan")
    foot = from_after(cells[:EDGE], "chan")

    def strip(cols):
        return jnp.concatenate([head[:, cols], cells[:, cols], foot[:, cols]], axis=0)

    left = from_before(strip(slice(tile_time - SIDE, tile_time)), "tm")
    right = from_after(strip(slice(0, SIDE)), "tm")
    where = jnp.stack(
        [lax.axis_index("chan") * tile_chan, lax.axis_index("tm") * tile_time]
    ).astype(jnp.int32)
    rows = 64
    ratio = rows // EDGE
    last = tile_chan // EDGE - 1
    whole = lambda i: (0, 0)
    return pl.pallas_call(
        tensor_kernel,
        grid=(tile_chan // rows,),
        in_specs=[
            pl.BlockSpec(memory_space=pltpu.SMEM),
            pl.BlockSpec((EDGE, tile_time), lambda i: (jnp.maximum(i * ratio - 1, 0), 0)),
            pl.BlockSpec((rows, tile_time), lambda i: (i, 0)),
            pl.BlockSpec((EDGE, tile_time), lambda i: (jnp.minimum((i + 1) * ratio, last), 0)),
            pl.BlockSpec((EDGE, tile_time), whole),
            pl.BlockSpec((EDGE, tile_time), whole),
            pl.BlockSpec((tile_chan + 2 * EDGE, SIDE), whole),
            pl.BlockSpec((tile_chan + 2 * EDGE, SIDE), whole),
        ],
        out_specs=pl.BlockSpec((rows, tile_time), lambda i: (i, 0)),
        out_shape=jax.ShapeDtypeStruct((tile_chan, tile_time), jnp.float32),
        compiler_params=pltpu.CompilerParams(vmem_limit_bytes=48 * 2**20),
        name="tensor_slowness",
    )(where, cells, cells, cells, head, foot, left, right)


def per_device(record, channel_ok, fan_bounds):
    chan_count = lax.axis_size("chan")
    time_count = lax.axis_size("tm")
    devices = chan_count * time_count
    tile_chan, tile_time = record.shape
    row_count = tile_chan // time_count
    half = TF // 2
    digits = TF // devices
    tiles = record * channel_ok.astype(jnp.bfloat16)[:, None]
    tiles = tiles.reshape(time_count, row_count, tile_time // TF, TF)
    first = (row_count // EDGE + 1) // 2 * EDGE
    series = [
        lax.all_to_all(part, "tm", split_axis=0, concat_axis=0)
        for part in (tiles[:, :first], tiles[:, first:])
    ]
    block_index = lax.axis_index("chan") * time_count + lax.axis_index("tm")
    ordered = fan_bounds[:, : NT // 2].reshape(2, half, TF).transpose(0, 2, 1)
    window = lax.dynamic_slice_in_dim(ordered, block_index * digits, digits, 1)
    bounds = step_bounds(window, fan_bounds[:, NT // 2])
    packed = (block_index == 0).astype(jnp.int32)[None]
    everyone = ("chan", "tm")
    pencils = []
    for part in series:
        spec = time_forward(part)
        spec = spec.reshape(devices, digits, spec.shape[1], TF)
        pencils.append(lax.all_to_all(spec, everyone, split_axis=0, concat_axis=0))
    rows = []
    for part in channel_filter(pencils, bounds, packed):
        back = lax.all_to_all(part, everyone, split_axis=0, concat_axis=0)
        lines = time_inverse(back.reshape(TF, back.shape[2], TF), time_count)
        rows.append(lax.all_to_all(lines, "tm", split_axis=0, concat_axis=0))
    rows = jnp.concatenate(rows, axis=1)
    return tensor_slowness(rows.reshape(tile_chan, tile_time))


def solution(mesh):
    in_specs = (P("chan", "tm"), P("chan"), P())
    out_specs = P("chan", "tm")
    return jax.shard_map(
        per_device, mesh=mesh, in_specs=in_specs, out_specs=out_specs, check_vma=False
    )
```
